32 devices in a mesh: seq: 8 (over y, x, core), head: 4 (over z).
Axes of the slice: x: 2, y: 2, z: 4, core: 2. Of those that a mesh axis runs over, the one named last changes fastest.
Arguments:
- queries: bfloat16 [128, 16384], P(None, 'head')
- cache_keys: bfloat16 [2, 32768, 1024], P(None, 'seq', 'head'), may hold values from -6 to 6
- cache_values: bfloat16 [2, 32768, 1024], P(None, 'seq', 'head'), may hold values from -6 to 6
- tree_keys: bfloat16 [128, 1024], P(None, 'head')
- tree_values: bfloat16 [128, 1024], P(None, 'head'), may hold values from -6 to 6
- ancestors: int32 [2, 64, 64], replicated, may hold values from 0 to 1, as said below
- filled_extents: int32 [2], replicated, may hold values from 1 to 32768, as said below
- out_weight: bfloat16 [16384, 16384], P('head', 'seq'), may hold values from -0.046875 to 0.046875
- residual: bfloat16 [128, 16384], P(None, 'seq'), may hold values from -6 to 6
- norm_gain: bfloat16 [16384], replicated, may hold values from 0.099609375 to 1.8984375
- vocab_weight: bfloat16 [16384, 65536], P(None, ('seq', 'head'))
- candidates: int32 [128], replicated, may hold values from 0 to 65535
- amateur: float32 [128], replicated, may hold values from -12 to -1
Outputs:
- hidden: bfloat16 [128, 16384], P(None, ('seq', 'head'))
- contrast: float32 [128], replicated
The draws below stay inside these ranges and needn't reach their ends.
Inputs may be any that keep to these rules, and one draw needn't show every extreme that they name: Rows are nodes; node 0 is the root; every node's parent has a smaller index; ancestors[b, i, i] = 1. Positions 0 to filled_extents[b] - 1 of request b are live; some request has length 32768.
All inputs are finite; a program needn't handle non-finite values.
Results may differ from the reference program's by a relative error of at most 0.006.
Values may be sent and summed in bfloat16 or wider, within the bound.
A program may use at most 256 MiB of HBM per device.

```python
import math
import jax
import jax.numpy as jnp
from jax import lax

REQUESTS = 2
NODES_REQ = 64
D = 16384
H = 128
KVH = 8
HD = 128
V = 65536
STORE_LIMIT = 32768
NODES = 128


def tree_key_base(key):
    return jax.random.normal(jax.random.fold_in(key, 11), (NODES, KVH * HD), jnp.float32)


def draw_tree_keys(key, part):
    return tree_key_base(key).astype(jnp.bfloat16)


def draw_queries(key, part):
    base = jax.random.normal(jax.random.fold_in(key, 12), (NODES, H * HD), jnp.float32)
    return base.astype(jnp.bfloat16)


def draw_vocab_weight(key, part):
    factor = 3.0 / math.sqrt(D)
    entries = jax.random.normal(jax.random.fold_in(key, 21), (D, V), jnp.float32) * factor
    return entries.astype(jnp.bfloat16)


def draw_filled_extents(key, part):
    drawn = jax.random.randint(jax.random.fold_in(key, 31), (REQUESTS,), 1, STORE_LIMIT + 1)
    longest = jax.random.randint(jax.random.fold_in(key, 32), (), 0, REQUESTS)
    return jnp.where(jnp.arange(REQUESTS, dtype=jnp.int32) == longest, STORE_LIMIT, drawn).astype(jnp.int32)


def draw_ancestors(key, part):
    index_row = jnp.arange(NODES_REQ, dtype=jnp.int32)
    raw_parent = jax.random.randint(jax.random.fold_in(key, 41), (REQUESTS, NODES_REQ), 0, NODES_REQ)
    parent = jnp.where(index_row[None, :] > 0, raw_parent % jnp.maximum(index_row[None, :], 1), 0).astype(jnp.int32)
    start_mask = jnp.broadcast_to(jnp.eye(NODES_REQ, dtype=jnp.int32)[None], (REQUESTS, NODES_REQ, NODES_REQ))

    def extend(node, table):
        parent_now = lax.dynamic_slice_in_dim(parent, node, 1, 1)[:, 0]
        where_from = jnp.broadcast_to(parent_now[:, None, None], (REQUESTS, 1, NODES_REQ))
        inherited = jnp.take_along_axis(table, where_from, axis=1)[:, 0, :]
        new_row = inherited + (index_row == node).astype(jnp.int32)[None, :]
        return lax.dynamic_update_slice_in_dim(table, new_row[:, None, :], node, 1)
    return lax.fori_loop(1, NODES_REQ, extend, start_mask)


def place_ends(array, key, low, top_value):
    longest = array.shape.index(max(array.shape))
    spots = []
    for shift in (0, 1):
        where = [jax.random.randint(jax.random.fold_in(key, axis), (), 0, length) for axis, length in enumerate(array.shape)]
        where[longest] = (where[longest] + shift) % array.shape[longest]
        spots.append(tuple(where))
    return array.at[spots[0]].set(low).at[spots[1]].set(top_value)


def block_levels(own_key, dims, cuts, smallest, largest):
    def one(position, blocks):
        draws = jax.random.uniform(jax.random.fold_in(jax.random.fold_in(own_key, 6), position), (blocks,), jnp.float32, smallest / len(cuts), largest / len(cuts))
        return jnp.repeat(jnp.exp(draws), dims[position] // blocks).reshape((-1,) + (1,) * (len(dims) - position - 1))

    level = one(*cuts[0])
    for cut in cuts[1:]:
        level = level * one(*cut)
    return level


def gaussian(own_key, shape, width, most, cuts=(), held_as=jnp.bfloat16):
    level = block_levels(own_key, shape, cuts, -0.22, 0.18) if cuts else 1.0
    result = jax.random.normal(own_key, shape, jnp.float32) * width * level
    return jnp.minimum(jnp.maximum(result, -most), most).astype(held_as)


def setup_inputs(seed: int = 0) -> dict:
    keys = jax.random.split(jax.random.key(seed), 14)
    return {
        "queries": draw_queries(jax.random.fold_in(keys[13], 71), 0),
        "cache_keys": gaussian(keys[1], (REQUESTS, STORE_LIMIT, KVH * HD), 1.0, 6.0, ((1, 8), (2, 4))),
        "cache_values": gaussian(keys[2], (REQUESTS, STORE_LIMIT, KVH * HD), 1.0, 6.0, ((1, 8), (2, 4))),
        "tree_keys": draw_tree_keys(jax.random.fold_in(keys[13], 71), 0),
        "tree_values": gaussian(keys[4], (NODES, KVH * HD), 1.0, 6.0, ((1, 4),)),
        "ancestors": draw_ancestors(jax.random.fold_in(keys[13], 71), 0),
        "filled_extents": draw_filled_extents(jax.random.fold_in(keys[13], 71), 0),
        "out_weight": gaussian(keys[7], (H * HD, D), (H * HD) ** -0.5, 0.046875, ((0, 4), (1, 8))),
        "residual": gaussian(keys[8], (NODES, D), 1.0, 6.0, ((1, 8),)),
        "norm_gain": jnp.clip(1.0 + 0.18 * jax.random.normal(keys[9], (D,), jnp.float32), 0.099609375, 1.8984375).astype(jnp.bfloat16),
        "vocab_weight": draw_vocab_weight(jax.random.fold_in(keys[13], 71), 0),
        "candidates": place_ends(jax.random.randint(keys[11], (NODES,), 0, V), jax.random.fold_in(keys[11], 1), 0, V - 1).astype(jnp.int32),
        "amateur": jnp.clip(jax.random.uniform(keys[12], (NODES,), jnp.float32, -12.0, -1.0), -12.0, -1.0),
    }


NEG_FILL = -1e+30
EPSILON = 1e-05
HIGH = lax.Precision.HIGHEST

def separate_channel_blend(asking_embeddings, stored_lookup_entries, stored_content_entries, guessed_branch_lookups, guessed_branch_contents, entry_validity, lineage_visibility_filter):
    score_scale = HD ** (-0.5)
    query_f = asking_embeddings.astype(jnp.float32)
    cached = jnp.einsum('ngd,pd->gnp', query_f, stored_lookup_entries.astype(jnp.float32), precision=HIGH) * score_scale
    local_tree = jnp.einsum('ngd,jd->gnj', query_f, guessed_branch_lookups.astype(jnp.float32), precision=HIGH) * score_scale
    valid_stored_indices = entry_validity[None, None, :]
    live_t = (lineage_visibility_filter > 0)[None, :, :]
    cached = jnp.where(valid_stored_indices, cached, NEG_FILL)
    local_tree = jnp.where(live_t, local_tree, NEG_FILL)
    highest = jnp.maximum(cached.max(-1), local_tree.max(-1))
    weight_c = jnp.where(valid_stored_indices, jnp.exp(cached - highest[..., None]), 0.0)
    weight_t = jnp.where(live_t, jnp.exp(local_tree - highest[..., None]), 0.0)
    weight_sum = weight_c.sum(-1) + weight_t.sum(-1)
    summed = jnp.einsum('gnp,pd->gnd', weight_c.astype(jnp.bfloat16).astype(jnp.float32), stored_content_entries.astype(jnp.float32), precision=HIGH)
    summed = summed + jnp.einsum('gnj,jd->gnd', weight_t.astype(jnp.bfloat16).astype(jnp.float32), guessed_branch_contents.astype(jnp.float32), precision=HIGH)
    return summed / weight_sum[..., None]

def reference(queries, cache_keys, cache_values, tree_keys, tree_values, ancestors, filled_extents, out_weight, residual, norm_gain, vocab_weight, candidates, amateur):
    group_size = H // KVH

    def one_item(item):
        sequence_ordinal = (item // KVH).astype(jnp.int32)
        kv_head = (item % KVH).astype(jnp.int32)
        row0 = (sequence_ordinal * NODES_REQ).astype(jnp.int32)
        asking_embeddings = lax.dynamic_slice(queries, (row0, (kv_head * group_size * HD).astype(jnp.int32)), (NODES_REQ, group_size * HD)).reshape(NODES_REQ, group_size, HD)
        zero = jnp.zeros((), jnp.int32)
        stored_lookup_entries = lax.dynamic_slice(cache_keys, (sequence_ordinal, zero, (kv_head * HD).astype(jnp.int32)), (1, STORE_LIMIT, HD))[0]
        stored_content_entries = lax.dynamic_slice(cache_values, (sequence_ordinal, zero, (kv_head * HD).astype(jnp.int32)), (1, STORE_LIMIT, HD))[0]
        guessed_branch_lookups = lax.dynamic_slice(tree_keys, (row0, (kv_head * HD).astype(jnp.int32)), (NODES_REQ, HD))
        guessed_branch_contents = lax.dynamic_slice(tree_values, (row0, (kv_head * HD).astype(jnp.int32)), (NODES_REQ, HD))
        entry_validity = jnp.arange(STORE_LIMIT, dtype=jnp.int32) < filled_extents[sequence_ordinal]
        lineage_visibility_filter = ancestors[sequence_ordinal]
        blended_result_matrix = separate_channel_blend(asking_embeddings, stored_lookup_entries, stored_content_entries, guessed_branch_lookups, guessed_branch_contents, entry_validity, lineage_visibility_filter)
        return blended_result_matrix.transpose(1, 0, 2).reshape(NODES_REQ, group_size * HD)
    pieces = lax.map(one_item, jnp.arange(REQUESTS * KVH, dtype=jnp.int32))
    attended = pieces.reshape(REQUESTS, KVH, NODES_REQ, group_size * HD).transpose(0, 2, 1, 3).reshape(NODES, H * HD).astype(jnp.bfloat16)
    projected = jnp.dot(attended, out_weight, preferred_element_type=jnp.float32)
    hidden = (residual.astype(jnp.float32) + projected).astype(jnp.bfloat16)
    hidden_f = hidden.astype(jnp.float32)
    mean_sq = lax.optimization_barrier(jnp.mean(hidden_f * hidden_f, axis=1))
    normed = (hidden_f * lax.rsqrt(mean_sq + EPSILON)[:, None] * norm_gain.astype(jnp.float32)).astype(jnp.bfloat16)
    logits = jnp.dot(normed, vocab_weight, preferred_element_type=jnp.float32)
    peak_logit = logits.max(axis=1)
    log_total = peak_logit + jnp.log(lax.optimization_barrier(jnp.sum(jnp.exp(logits - peak_logit[:, None]), axis=1)))
    chosen = jnp.take_along_axis(logits, candidates[:, None].astype(jnp.int32), axis=1)[:, 0]
    contrast = chosen - log_total - amateur
    return (hidden, contrast)
```

```python
import functools
import math

import jax
import jax.numpy as jnp
from jax import lax
from jax.experimental import pallas as pl
from jax.experimental.pallas import tpu as pltpu
from jax.sharding import PartitionSpec as P

HD = 128
NEG_FILL = -1e30
EPSILON = 1e-05
MESH = pl.DeviceIdType.MESH
EXP2_SCALE = HD ** (-0.5) * math.log2(math.e)
LANES = 256


def attention_kernel(
    meta_ref, q_ref, k_ref, v_ref, tk_ref, tv_ref, tm_ref, acc_ref, st_ref, q_t, o_t, top, total
):
    b = pl.program_id(0)
    p = pl.program_id(2)
    block = k_ref.shape[1]
    rows = q_t.shape[1]

    @pl.when(p == 0)
    def _():
        for g in range(0, q_ref.shape[1], 2 * HD):
            pair = jnp.concatenate([q_ref[:, g : g + HD], q_ref[:, g + HD : g + 2 * HD]], axis=0)
            q_t[:, g // 2 : g // 2 + HD] = pair.astype(jnp.float32).T.astype(jnp.bfloat16)
        top[...] = jnp.full_like(top, NEG_FILL)
        total[...] = jnp.zeros_like(total)
        o_t[...] = jnp.zeros_like(o_t)

    def step(keys, values, live):
        values_t = values.T
        for c in range(0, rows, LANES):
            cols = slice(c, c + LANES)
            s = jnp.dot(keys, q_t[:, cols], preferred_element_type=jnp.float32)
            if live is not None:
                s = jnp.where(live(), s, NEG_FILL)
            before = top[:, cols]
            now = jnp.maximum(before, s.max(axis=0, keepdims=True) * EXP2_SCALE)
            w = jnp.exp2(s * EXP2_SCALE - now)
            factor = jnp.exp2(before - now)
            top[:, cols] = now
            total[:, cols] = total[:, cols] * factor + w.sum(axis=0, keepdims=True)
            o_t[:, cols] = o_t[:, cols] * factor + jnp.dot(
                values_t, w.astype(jnp.bfloat16), preferred_element_type=jnp.float32
            )

    left = meta_ref[b] - p * block

    @pl.when(left >= block)
    def _():
        step(k_ref[0], v_ref[0], None)

    @pl.when((left > 0) & (left < block))
    def _():
        step(
            k_ref[0],
            v_ref[0],
            lambda: lax.broadcasted_iota(jnp.int32, (block, LANES), 0) < left,
        )

    @pl.when(p == pl.num_programs(2) - 1)
    def _():
        @pl.when(meta_ref[pl.num_programs(0)] > 0)
        def _():
            step(tk_ref[...], tv_ref[...], lambda: tm_ref[0] > 0)

        width = acc_ref.shape[2]
        for i in range(acc_ref.shape[0]):
            cols = slice(i * width, (i + 1) * width)
            acc_ref[i] = o_t[:, cols].astype(jnp.bfloat16)
            row = lax.broadcasted_iota(jnp.int32, (8, width), 0)
            st_ref[i] = jnp.where(row == 0, top[:, cols], total[:, cols])


def attention(queries, keys, values, tree_keys, tree_values, ancestors, extents, seq):
    requests, positions, kv_width = keys.shape
    kv = kv_width // HD
    nodes = queries.shape[0] // requests
    group = queries.shape[1] // kv // HD
    rows = group * nodes
    pieces = seq // (requests * kv)
    width = rows // pieces
    block = min(1024, positions)
    me = lax.axis_index("seq")
    live = jnp.clip(extents - me * positions, 0, positions)
    meta = jnp.concatenate([live, (me == seq - 1).astype(jnp.int32)[None]])
    mask = jnp.tile(ancestors.transpose(0, 2, 1), (1, 1, LANES // nodes))
    cells = requests * kv * rows * positions
    return pl.pallas_call(
        attention_kernel,
        grid_spec=pltpu.PrefetchScalarGridSpec(
            num_scalar_prefetch=1,
            grid=(requests, kv, positions // block),
            in_specs=[
                pl.BlockSpec((nodes, group * HD), lambda b, g, p, m: (b, g)),
                pl.BlockSpec((1, block, HD), lambda b, g, p, m: (b, p, g)),
                pl.BlockSpec((1, block, HD), lambda b, g, p, m: (b, p, g)),
                pl.BlockSpec((nodes, HD), lambda b, g, p, m: (b, g)),
                pl.BlockSpec((nodes, HD), lambda b, g, p, m: (b, g)),
                pl.BlockSpec((1, nodes, LANES), lambda b, g, p, m: (b, 0, 0)),
            ],
            out_specs=[
                pl.BlockSpec((pieces, HD, width), lambda b, g, p, m: (b * kv + g, 0, 0)),
                pl.BlockSpec((pieces, 8, width), lambda b, g, p, m: (b * kv + g, 0, 0)),
            ],
            scratch_shapes=[
                pltpu.VMEM((HD, rows), jnp.bfloat16),
                pltpu.VMEM((HD, rows), jnp.float32),
                pltpu.VMEM((1, rows), jnp.float32),
                pltpu.VMEM((1, rows), jnp.float32),
            ],
        ),
        out_shape=[
            jax.ShapeDtypeStruct((seq, HD, width), jnp.bfloat16),
            jax.ShapeDtypeStruct((seq, 8, width), jnp.float32),
        ],
        compiler_params=pltpu.CompilerParams(vmem_limit_bytes=40 * 2**20),
        cost_estimate=pl.CostEstimate(
            flops=4 * HD * cells,
            bytes_accessed=4 * requests * positions * kv_width,
            transcendentals=cells,
        ),
    )(meta, queries, keys, values, tree_keys, tree_values, mask)


def toggled(index, flips, size):
    out = 0
    bit = 1
    while bit < size:
        out = out + ((index // bit + (flips // bit) % 2) % 2) * bit
        bit *= 2
    return out


def tail_kernel(
    seq, head, slots, nodes,
    acc_hbm, st_hbm, wo_hbm, res_ref, gain_ref, voc_hbm, cand_ref, amateur_ref,
    hid_ref, con_ref,
    racc, rst, att, wo, voc, psend, precv, hg, lacc, vst1, vst2,
    own_sem, wo_sem, voc_sem,
    acc_ss, acc_rs, st_ss, st_rs, att_ss, att_rs, p_ss, p_rs,
    z_ss, z_rs, c_ss, c_rs, t_ss, t_rs, v1_ss, v1_rs, v2_ss, v2_rs,
):
    s = lax.axis_index("seq")
    h = lax.axis_index("head")
    chips = seq // 2
    chip, core = s // 2, s % 2
    depth, share = wo.shape[1], wo.shape[2]
    cols = share * head
    vocab = voc_hbm.shape[1]
    width = racc.shape[2]
    pending = []

    def send(src, dst, ss, rs, to):
        copy = pltpu.make_async_remote_copy(
            src_ref=src, dst_ref=dst, send_sem=ss, recv_sem=rs, device_id=to, device_id_type=MESH
        )
        copy.start()
        pending.append(copy)
        return copy

    own_acc = pltpu.make_async_copy(acc_hbm.at[s], racc.at[0], own_sem.at[0])
    own_st = pltpu.make_async_copy(st_hbm.at[s], rst.at[0], own_sem.at[1])
    own_acc.start()
    own_st.start()

    def seq_peer(k):
        return (s + k) % seq

    def head_peer(k):
        return (h + k) % head

    barrier = pltpu.get_barrier_semaphore()
    for k in range(1, seq):
        pl.semaphore_signal(barrier, inc=1, device_id={"seq": seq_peer(k)}, device_id_type=MESH)
    for k in range(1, head):
        pl.semaphore_signal(barrier, inc=1, device_id={"head": head_peer(k)}, device_id_type=MESH)
    pl.semaphore_wait(barrier, seq + head - 2)

    acc_copies = []
    for k in range(1, seq):
        to = seq_peer(k)
        acc_copies.append(
            (
                send(st_hbm.at[to], rst.at[k], st_ss.at[k], st_rs.at[k], {"seq": to}),
                send(acc_hbm.at[to], racc.at[k], acc_ss.at[k], acc_rs.at[k], {"seq": to}),
            )
        )

    wo_copies = {}
    for k in list(range(1, head)) + [0]:
        start = pl.multiple_of(head_peer(k) * share, 128)
        wo_copies[k] = pltpu.make_async_copy(
            wo_hbm.at[:, pl.ds(start, share)], wo.at[k], wo_sem.at[k]
        )
        wo_copies[k].start()

    order = [(kc, e, i) for kc in range(chips) for e in range(2) for i in range(head // 2)]

    def voc_copies(t):
        kc, e, i = order[t]
        source = toggled(chip, kc, chips) * 2 + (core + e) % 2
        out = []
        for j in range(2):
            hs = (h + head - (2 * i + j)) % head
            row = pl.multiple_of(source * cols + hs * share, 128)
            out.append(
                pltpu.make_async_copy(
                    voc_hbm.at[pl.ds(row, share)],
                    voc.at[t % slots, pl.ds(j * share, share)],
                    voc_sem.at[t % slots, j],
                )
            )
        return out

    for t in range(min(slots, len(order))):
        for copy in voc_copies(t):
            copy.start()

    own_st.wait()
    own_acc.wait()
    for st, acc in acc_copies:
        st.wait_recv()
        acc.wait_recv()
    highest = rst[0, 0:1, :]
    for k in range(1, seq):
        highest = jnp.maximum(highest, rst[k, 0:1, :])
    number = jnp.zeros((HD, width), jnp.float32)
    weight = jnp.zeros((1, width), jnp.float32)
    for k in range(seq):
        factor = jnp.exp2(rst[k, 0:1, :] - highest)
        weight = weight + rst[k, 1:2, :] * factor
        number = number + racc[k].astype(jnp.float32) * factor
    mean = (number / weight).T
    row0 = pl.multiple_of((s // (seq // 2)) * nodes, nodes)
    wide = width // nodes * HD
    col0 = pl.multiple_of((s % (seq // 2)) * wide, 128)
    part = att.at[pl.ds(row0, nodes), pl.ds(col0, wide)]
    part[...] = jnp.concatenate(
        [mean[i : i + nodes] for i in range(0, width, nodes)], axis=1
    ).astype(jnp.bfloat16)
    att_copies = [
        send(part, part, att_ss.at[k], att_rs.at[k], {"seq": seq_peer(k)}) for k in range(1, seq)
    ]
    for copy in att_copies:
        copy.wait_recv()

    p_copies = []
    for k in list(range(1, head)) + [0]:
        wo_copies[k].wait()
        product = jnp.dot(att[...], wo[k], preferred_element_type=jnp.float32)
        if k:
            psend[k] = product.astype(jnp.bfloat16)
            p_copies.append(
                send(psend.at[k], precv.at[k], p_ss.at[k], p_rs.at[k], {"head": head_peer(k)})
            )
    for copy in p_copies:
        copy.wait_recv()
    for k in range(1, head):
        product = product + precv[k].astype(jnp.float32)
    mine = pl.ds(pl.multiple_of(h * share, 128), share)
    hidden = (res_ref[:, mine].astype(jnp.float32) + product).astype(jnp.bfloat16)
    hid_ref[...] = hidden
    hg[0, 0, 0] = hidden

    def spread(hr):
        piece = hg.at[0, 0, hr]
        out = {}
        for kc in range(1, chips):
            to = toggled(chip, kc, chips) * 2 + core
            out[kc] = send(
                piece, hg.at[kc, 0, hr], c_ss.at[kc, hr], c_rs.at[kc, hr], {"seq": to}
            )
        out[0] = to_partner(0, hr)
        return out

    def to_partner(kc, hr):
        return send(
            hg.at[kc, 0, hr],
            hg.at[kc, 1, hr],
            t_ss.at[kc, hr],
            t_rs.at[kc, hr],
            {"seq": chip * 2 + (core + 1) % 2},
        )

    z_copies = [
        send(hg.at[0, 0, 0], hg.at[0, 0, k], z_ss.at[k], z_rs.at[k], {"head": head_peer(k)})
        for k in range(1, head)
    ]
    spreads = [spread(0)]
    for hr in range(1, head):
        z_copies[hr - 1].wait_recv()
        spreads.append(spread(hr))
    partner = {0: [out[0] for out in spreads]}

    def forward(kc):
        partner[kc] = []
        for hr in range(head):
            spreads[hr][kc].wait_recv()
            partner[kc].append(to_partner(kc, hr))

    squares = jnp.zeros((hg.shape[3], 1), jnp.float32)
    lacc[...] = jnp.zeros_like(lacc)
    tile = min(512, vocab)
    done = 0
    for kc in range(chips):
        for e in range(2):
            if done + 1 < chips:
                forward(done + 1)
            done += 1
            if e == 1:
                for copy in partner[kc]:
                    copy.wait_recv()
            source = toggled(chip, kc, chips) * 2 + (core + e) % 2
            for i in range(head // 2):
                t = (kc * 2 + e) * (head // 2) + i
                parts = []
                for j in range(2):
                    hr = 2 * i + j
                    hs = (h + head - hr) % head
                    at = pl.multiple_of(source * cols + hs * share, 128)
                    x = hg[kc, e, hr].astype(jnp.float32)
                    squares = squares + jnp.sum(x * x, axis=1, keepdims=True)
                    gain = gain_ref[:, pl.ds(at, share)].astype(jnp.float32)
                    parts.append((x * gain).astype(jnp.bfloat16))
                x = jnp.concatenate(parts, axis=1)
                for copy in voc_copies(t):
                    copy.wait()

                @pl.loop(0, vocab // tile)
                def _(n):
                    span = pl.ds(pl.multiple_of(n * tile, 128), tile)
                    lacc[:, span] += jnp.dot(
                        x, voc[t % slots, :, span], preferred_element_type=jnp.float32
                    )

                if t + slots < len(order):
                    for copy in voc_copies(t + slots):
                        copy.start()

    logits = lacc[...] * lax.rsqrt(squares / (cols * seq) + EPSILON)
    peak = logits.max(axis=1, keepdims=True)
    mass = jnp.sum(jnp.exp(logits - peak), axis=1, keepdims=True)
    column = lax.broadcasted_iota(jnp.int32, logits.shape, 1) + (s * head + h) * vocab
    chosen = jnp.sum(jnp.where(column == cand_ref[...], logits, 0.0), axis=1, keepdims=True)
    lane = lax.broadcasted_iota(jnp.int32, (logits.shape[0], 128), 1)
    packed = jnp.where(lane == 0, peak, jnp.where(lane == 1, mass, chosen)).T
    vst1[0] = packed[0:8]

    def merged(ref, count):
        top = ref[0, 0:1, :]
        for k in range(1, count):
            top = jnp.maximum(top, ref[k, 0:1, :])
        total = jnp.zeros_like(top)
        picked = jnp.zeros_like(top)
        for k in range(count):
            total = total + ref[k, 1:2, :] * jnp.exp(ref[k, 0:1, :] - top)
            picked = picked + ref[k, 2:3, :]
        return top, total, picked

    copies = [
        send(vst1.at[0], vst1.at[k], v1_ss.at[k], v1_rs.at[k], {"seq": seq_peer(k)})
        for k in range(1, seq)
    ]
    for copy in copies:
        copy.wait_recv()
    top, total, picked = merged(vst1, seq)
    row = lax.broadcasted_iota(jnp.int32, (8, 128), 0)
    vst2[0] = jnp.where(row == 0, top, jnp.where(row == 1, total, picked))
    copies = [
        send(vst2.at[0], vst2.at[k], v2_ss.at[k], v2_rs.at[k], {"head": head_peer(k)})
        for k in range(1, head)
    ]
    for copy in copies:
        copy.wait_recv()
    top, total, picked = merged(vst2, head)
    con_ref[...] = picked - (top + jnp.log(total)) - amateur_ref[...]
    for copy in pending:
        copy.wait_send()


def tail(acc, stats, out_weight, residual, norm_gain, vocab_weight, candidates, amateur, head):
    seq, _, width = acc.shape
    depth, cols = out_weight.shape
    share = cols // head
    vocab = vocab_weight.shape[1]
    count = residual.shape[0]
    nodes = count // 2
    chips = seq // 2
    slots = min(7, seq * head // 2)
    dma = pltpu.SemaphoreType.DMA
    vmem = pl.BlockSpec(memory_space=pltpu.VMEM)
    hbm = pl.BlockSpec(memory_space=pl.ANY)
    bf16, f32 = jnp.bfloat16, jnp.float32
    hidden, contrast = pl.pallas_call(
        functools.partial(tail_kernel, seq, head, slots, nodes),
        in_specs=[hbm, hbm, hbm, vmem, vmem, hbm, vmem, vmem],
        out_specs=[vmem, vmem],
        out_shape=[
            jax.ShapeDtypeStruct((count, share), bf16),
            jax.ShapeDtypeStruct((1, count), f32),
        ],
        scratch_shapes=[
            pltpu.VMEM((seq, HD, width), bf16),
            pltpu.VMEM((seq, 8, width), f32),
            pltpu.VMEM((count, depth), bf16),
            pltpu.VMEM((head, depth, share), bf16),
            pltpu.VMEM((slots, 2 * share, vocab), bf16),
            pltpu.VMEM((head, count, share), bf16),
            pltpu.VMEM((head, count, share), bf16),
            pltpu.VMEM((chips, 2, head, count, share), bf16),
            pltpu.VMEM((count, vocab), f32),
            pltpu.VMEM((seq, 8, 128), f32),
            pltpu.VMEM((head, 8, 128), f32),
            dma((2,)), dma((head,)), dma((slots, 2)),
            dma((seq,)), dma((seq,)), dma((seq,)), dma((seq,)),
            dma((seq,)), dma((seq,)), dma((head,)), dma((head,)),
            dma((head,)), dma((head,)),
            dma((chips, head)), dma((chips, head)), dma((chips, head)), dma((chips, head)),
            dma((seq,)), dma((seq,)), dma((head,)), dma((head,)),
        ],
        compiler_params=pltpu.CompilerParams(
            collective_id=0, has_side_effects=True, vmem_limit_bytes=60 * 2**20
        ),
        cost_estimate=pl.CostEstimate(
            flops=2 * count * (depth * cols + vocab_weight.size),
            bytes_accessed=2 * (out_weight.size + vocab_weight.size),
            transcendentals=count * vocab,
        ),
    )(
        acc, stats, out_weight, residual, norm_gain[None, :], vocab_weight,
        candidates[:, None], amateur[None, :],
    )
    return hidden, contrast[0]


def solution(mesh):
    seq, head = mesh.shape["seq"], mesh.shape["head"]

    def body(
        queries, cache_keys, cache_values, tree_keys, tree_values, ancestors, filled_extents,
        out_weight, residual, norm_gain, vocab_weight, candidates, amateur,
    ):
        acc, stats = attention(
            queries, cache_keys, cache_values, tree_keys, tree_values, ancestors,
            filled_extents, seq,
        )
        return tail(
            acc, stats, out_weight, residual, norm_gain, vocab_weight, candidates, amateur, head
        )

    in_specs = (
        P(None, "head"),
        P(None, "seq", "head"),
        P(None, "seq", "head"),
        P(None, "head"),
        P(None, "head"),
        P(),
        P(),
        P("head", "seq"),
        P(None, "seq"),
        P(),
        P(None, ("seq", "head")),
        P(),
        P(),
    )
    out_specs = (P(None, ("seq", "head")), P())
    return jax.shard_map(body, mesh=mesh, in_specs=in_specs, out_specs=out_specs, check_vma=False)
```

```python
import functools
import math

import jax
import jax.numpy as jnp
from jax import lax
from jax.experimental import pallas as pl
from jax.experimental.pallas import tpu as pltpu
from jax.sharding import PartitionSpec as P

HD = 128
NEG_FILL = -1e30
EPSILON = 1e-05
MESH = pl.DeviceIdType.MESH
EXP2_SCALE = HD ** (-0.5) * math.log2(math.e)
LANES = 256
SUM_ROWS = 16
WEIGHT_TYPE = jnp.bfloat16


def attention_kernel(
    meta_ref, q_ref, k_ref, v_ref, tk_ref, tv_ref, tm_ref, acc_ref, st_ref, q_t, o_t, top
):
    b = pl.program_id(0)
    p = pl.program_id(2)
    block = k_ref.shape[1]
    rows = q_t.shape[1]

    @pl.when(p == 0)
    def _():
        for g in range(0, q_ref.shape[1], 2 * HD):
            pair = jnp.concatenate([q_ref[:, g : g + HD], q_ref[:, g + HD : g + 2 * HD]], axis=0)
            q_t[:, g // 2 : g // 2 + HD] = pair.astype(jnp.float32).T.astype(jnp.bfloat16)
        top[...] = jnp.full_like(top, NEG_FILL)
        o_t[...] = jnp.zeros_like(o_t)

    def step(keys, values, live):
        values_t = jnp.concatenate(
            [values.T, jnp.ones((SUM_ROWS, values.shape[0]), jnp.bfloat16)], axis=0
        )

        def scored(c):
            s = jnp.dot(keys, q_t[:, c : c + LANES], preferred_element_type=jnp.float32)
            if live is not None:
                s = jnp.where(live(), s, NEG_FILL)
            return s

        ahead = scored(0)
        late = None
        for c in range(0, rows + LANES, LANES):
            s = ahead
            if c + LANES < rows:
                ahead = scored(c + LANES)
            if late is not None:
                cols, factor, w = late
                o_t[:, cols] = o_t[:, cols] * factor + jnp.dot(
                    values_t, w, preferred_element_type=jnp.float32
                )
            if c < rows:
                cols = slice(c, c + LANES)
                before = top[:, cols]
                now = jnp.maximum(before, s.max(axis=0, keepdims=True) * EXP2_SCALE)
                w = jnp.exp2((s * EXP2_SCALE - now).astype(WEIGHT_TYPE)).astype(jnp.bfloat16)
                top[:, cols] = now
                late = (cols, jnp.exp2(before - now), w)

    left = meta_ref[b] - p * block

    @pl.when(left >= block)
    def _():
        step(k_ref[0], v_ref[0], None)

    @pl.when((left > 0) & (left < block))
    def _():
        step(
            k_ref[0],
            v_ref[0],
            lambda: lax.broadcasted_iota(jnp.int32, (block, LANES), 0) < left,
        )

    @pl.when(p == pl.num_programs(2) - 1)
    def _():
        @pl.when(meta_ref[pl.num_programs(0)] > 0)
        def _():
            step(tk_ref[...], tv_ref[...], lambda: tm_ref[0] > 0)

        width = acc_ref.shape[2]
        for i in range(acc_ref.shape[0]):
            cols = slice(i * width, (i + 1) * width)
            acc_ref[i] = o_t[:HD, cols].astype(jnp.bfloat16)
            row = lax.broadcasted_iota(jnp.int32, (8, width), 0)
            st_ref[i] = jnp.where(row == 0, top[:, cols], o_t[HD : HD + 1, cols])


def attention(queries, keys, values, tree_keys, tree_values, ancestors, extents, seq):
    requests, positions, kv_width = keys.shape
    kv = kv_width // HD
    nodes = queries.shape[0] // requests
    group = queries.shape[1] // kv // HD
    rows = group * nodes
    pieces = seq // (requests * kv)
    width = rows // pieces
    block = min(1024, positions)
    me = lax.axis_index("seq")
    live = jnp.clip(extents - me * positions, 0, positions)
    meta = jnp.concatenate([live, (me == seq - 1).astype(jnp.int32)[None]])
    mask = jnp.tile(ancestors.transpose(0, 2, 1), (1, 1, LANES // nodes))
    cells = requests * kv * rows * positions
    return pl.pallas_call(
        attention_kernel,
        grid_spec=pltpu.PrefetchScalarGridSpec(
            num_scalar_prefetch=1,
            grid=(requests, kv, positions // block),
            in_specs=[
                pl.BlockSpec((nodes, group * HD), lambda b, g, p, m: (b, g)),
                pl.BlockSpec((1, block, HD), lambda b, g, p, m: (b, p, g)),
                pl.BlockSpec((1, block, HD), lambda b, g, p, m: (b, p, g)),
                pl.BlockSpec((nodes, HD), lambda b, g, p, m: (b, g)),
                pl.BlockSpec((nodes, HD), lambda b, g, p, m: (b, g)),
                pl.BlockSpec((1, nodes, LANES), lambda b, g, p, m: (b, 0, 0)),
            ],
            out_specs=[
                pl.BlockSpec((pieces, HD, width), lambda b, g, p, m: (b * kv + g, 0, 0)),
                pl.BlockSpec((pieces, 8, width), lambda b, g, p, m: (b * kv + g, 0, 0)),
            ],
            scratch_shapes=[
                pltpu.VMEM((HD, rows), jnp.bfloat16),
                pltpu.VMEM((HD + SUM_ROWS, rows), jnp.float32),
                pltpu.VMEM((1, rows), jnp.float32),
            ],
        ),
        out_shape=[
            jax.ShapeDtypeStruct((seq, HD, width), jnp.bfloat16),
            jax.ShapeDtypeStruct((seq, 8, width), jnp.float32),
        ],
        compiler_params=pltpu.CompilerParams(vmem_limit_bytes=60 * 2**20),
        cost_estimate=pl.CostEstimate(
            flops=4 * HD * cells,
            bytes_accessed=4 * requests * positions * kv_width,
            transcendentals=cells,
        ),
    )(meta, queries, keys, values, tree_keys, tree_values, mask)


def toggled(index, flips, size):
    out = 0
    bit = 1
    while bit < size:
        out = out + ((index // bit + (flips // bit) % 2) % 2) * bit
        bit *= 2
    return out


def tail_kernel(
    seq, head, slots, nodes,
    acc_hbm, st_hbm, wo_hbm, res_ref, gain_ref, voc_hbm, cand_ref, amateur_ref,
    hid_ref, con_ref,
    racc, rst, att, wo, voc, psend, precv, hg, lacc, vst1, vst2,
    own_sem, wo_sem, voc_sem,
    acc_ss, acc_rs, st_ss, st_rs, att_ss, att_rs, p_ss, p_rs,
    z_ss, z_rs, c_ss, c_rs, t_ss, t_rs, v1_ss, v1_rs, v2_ss, v2_rs,
):
    s = lax.axis_index("seq")
    h = lax.axis_index("head")
    chips = seq // 2
    chip, core = s // 2, s % 2
    depth, share = wo.shape[1], wo.shape[2]
    cols = share * head
    vocab = voc_hbm.shape[1]
    width = racc.shape[2]
    pending = []

    def send(src, dst, ss, rs, to):
        copy = pltpu.make_async_remote_copy(
            src_ref=src, dst_ref=dst, send_sem=ss, recv_sem=rs, device_id=to, device_id_type=MESH
        )
        copy.start()
        pending.append(copy)
        return copy

    own_acc = pltpu.make_async_copy(acc_hbm.at[s], racc.at[0], own_sem.at[0])
    own_st = pltpu.make_async_copy(st_hbm.at[s], rst.at[0], own_sem.at[1])
    own_acc.start()
    own_st.start()

    def seq_peer(k):
        return (s + k) % seq

    def head_peer(k):
        return (h + k) % head

    barrier = pltpu.get_barrier_semaphore()
    for k in range(1, seq):
        pl.semaphore_signal(barrier, inc=1, device_id={"seq": seq_peer(k)}, device_id_type=MESH)
    for k in range(1, head):
        pl.semaphore_signal(barrier, inc=1, device_id={"head": head_peer(k)}, device_id_type=MESH)
    pl.semaphore_wait(barrier, seq + head - 2)

    acc_copies = []
    for k in range(1, seq):
        to = seq_peer(k)
        acc_copies.append(
            (
                send(st_hbm.at[to], rst.at[k], st_ss.at[k], st_rs.at[k], {"seq": to}),
                send(acc_hbm.at[to], racc.at[k], acc_ss.at[k], acc_rs.at[k], {"seq": to}),
            )
        )

    wo_copies = {}
    for k in list(range(1, head)) + [0]:
        start = pl.multiple_of(head_peer(k) * share, 128)
        wo_copies[k] = pltpu.make_async_copy(
            wo_hbm.at[:, pl.ds(start, share)], wo.at[k], wo_sem.at[k]
        )
        wo_copies[k].start()

    steps = sorted(range(chips), key=lambda kc: (kc.bit_count(), kc))
    order = [(kc, e, i) for kc in steps for e in range(2) for i in range(head // 2)]

    def voc_copies(t):
        kc, e, i = order[t]
        source = toggled(chip, kc, chips) * 2 + (core + e) % 2
        out = []
        for j in range(2):
            hs = (h + head - (2 * i + j)) % head
            row = pl.multiple_of(source * cols + hs * share, 128)
            out.append(
                pltpu.make_async_copy(
                    voc_hbm.at[pl.ds(row, share)],
                    voc.at[t % slots, pl.ds(j * share, share)],
                    voc_sem.at[t % slots, j],
                )
            )
        return out

    for t in range(min(slots, len(order))):
        for copy in voc_copies(t):
            copy.start()

    own_st.wait()
    own_acc.wait()
    for st, acc in acc_copies:
        st.wait_recv()
        acc.wait_recv()
    highest = rst[0, 0:1, :]
    for k in range(1, seq):
        highest = jnp.maximum(highest, rst[k, 0:1, :])
    number = jnp.zeros((HD, width), jnp.float32)
    weight = jnp.zeros((1, width), jnp.float32)
    for k in range(seq):
        factor = jnp.exp2(rst[k, 0:1, :] - highest)
        weight = weight + rst[k, 1:2, :] * factor
        number = number + racc[k].astype(jnp.float32) * factor
    mean = (number / weight).T
    row0 = pl.multiple_of((s // (seq // 2)) * nodes, nodes)
    wide = width // nodes * HD
    col0 = pl.multiple_of((s % (seq // 2)) * wide, 128)
    part = att.at[pl.ds(row0, nodes), pl.ds(col0, wide)]
    part[...] = jnp.concatenate(
        [mean[i : i + nodes] for i in range(0, width, nodes)], axis=1
    ).astype(jnp.bfloat16)
    def att_part(source):
        row = pl.multiple_of((source // (seq // 2)) * nodes, nodes)
        col = pl.multiple_of((source % (seq // 2)) * wide, 128)
        return att.at[pl.ds(row, nodes), pl.ds(col, wide)]

    def att_send(source, k, to):
        piece = att_part(source)
        return send(piece, piece, att_ss.at[k], att_rs.at[k], {"seq": to})

    other = chip * 2 + (core + 1) % 2
    att_copies = [
        att_send(s, 2 * kc, toggled(chip, kc, chips) * 2 + core) for kc in range(1, chips)
    ]
    att_swaps = [att_send(s, 1, other)]
    for kc in range(1, chips):
        source = toggled(chip, kc, chips) * 2 + core
        arrived = att_part(source)
        pltpu.make_async_remote_copy(
            src_ref=arrived, dst_ref=arrived, send_sem=att_ss.at[2 * kc],
            recv_sem=att_rs.at[2 * kc], device_id={"seq": source}, device_id_type=MESH,
        ).wait_recv()
        att_swaps.append(att_send(source, 2 * kc + 1, other))
    for copy in att_swaps:
        copy.wait_recv()

    p_copies = []
    for k in list(range(1, head)) + [0]:
        wo_copies[k].wait()
        product = jnp.dot(att[...], wo[k], preferred_element_type=jnp.float32)
        if k:
            psend[k] = product.astype(jnp.bfloat16)
            p_copies.append(
                send(psend.at[k], precv.at[k], p_ss.at[k], p_rs.at[k], {"head": head_peer(k)})
            )
    for copy in p_copies:
        copy.wait_recv()
    for k in range(1, head):
        product = product + precv[k].astype(jnp.float32)
    mine = pl.ds(pl.multiple_of(h * share, 128), share)
    hidden = (res_ref[:, mine].astype(jnp.float32) + product).astype(jnp.bfloat16)
    hid_ref[...] = hidden
    hg[0, 0, 0] = hidden

    bits = [1 << i for i in range(chips.bit_length() - 1)]
    near = {}
    partner = {}

    def parent(kc, hr):
        held = [bit for bit in bits if kc & bit]
        return kc ^ (held[0] if hr % 2 == 0 else held[-1])

    def spread(kc, hr):
        piece = hg.at[kc, 0, hr]
        for bit in bits:
            child = kc ^ bit
            if child > kc and parent(child, hr) == kc:
                near[child, hr] = send(
                    piece,
                    hg.at[child, 0, hr],
                    c_ss.at[child, hr],
                    c_rs.at[child, hr],
                    {"seq": toggled(chip, bit, chips) * 2 + core},
                )
        partner[kc, hr] = send(
            piece, hg.at[kc, 1, hr], t_ss.at[kc, hr], t_rs.at[kc, hr], {"seq": other}
        )

    def relay(kc, hr):
        near[kc, hr].wait_recv()
        spread(kc, hr)

    z_copies = [
        send(hg.at[0, 0, 0], hg.at[0, 0, k], z_ss.at[k], z_rs.at[k], {"head": head_peer(k)})
        for k in range(1, head)
    ]
    spread(0, 0)
    for hr in range(1, head):
        z_copies[hr - 1].wait_recv()
        spread(0, hr)
        for bit in bits:
            relay(bit, hr - 1)
    late = sorted(kc for kc in range(1, chips) if kc not in bits)

    squares = jnp.zeros((hg.shape[3], 1), jnp.float32)
    lacc[...] = jnp.zeros_like(lacc)
    tile = min(512, vocab)
    rank = 0
    for kc in steps:
        for e in range(2):
            if rank == 1:
                for bit in bits:
                    relay(bit, head - 1)
            if rank >= 2:
                for _ in range(-(-len(late) // (len(bits) * 2))):
                    if late:
                        done = late.pop(0)
                        for hr in range(head):
                            relay(done, hr)
            rank += 1
            if e == 1:
                for hr in range(head):
                    partner[kc, hr].wait_recv()
            source = toggled(chip, kc, chips) * 2 + (core + e) % 2
            for i in range(head // 2):
                t = order.index((kc, e, i))
                parts = []
                for j in range(2):
                    hr = 2 * i + j
                    hs = (h + head - hr) % head
                    at = pl.multiple_of(source * cols + hs * share, 128)
                    x = hg[kc, e, hr].astype(jnp.float32)
                    squares = squares + jnp.sum(x * x, axis=1, keepdims=True)
                    gain = gain_ref[:, pl.ds(at, share)].astype(jnp.float32)
                    parts.append((x * gain).astype(jnp.bfloat16))
                x = jnp.concatenate(parts, axis=1)
                for copy in voc_copies(t):
                    copy.wait()

                @pl.loop(0, vocab // tile)
                def _(n):
                    span = pl.ds(pl.multiple_of(n * tile, 128), tile)
                    lacc[:, span] += jnp.dot(
                        x, voc[t % slots, :, span], preferred_element_type=jnp.float32
                    )

                if t + slots < len(order):
                    for copy in voc_copies(t + slots):
                        copy.start()

    logits = lacc[...] * lax.rsqrt(squares / (cols * seq) + EPSILON)
    peak = logits.max(axis=1, keepdims=True)
    mass = jnp.sum(jnp.exp(logits - peak), axis=1, keepdims=True)
    count = logits.shape[0]
    cand = jnp.broadcast_to(cand_ref[...].astype(jnp.float32), (count, count)).T
    cand = cand[:, 0:1].astype(jnp.int32)
    column = lax.broadcasted_iota(jnp.int32, logits.shape, 1) + (s * head + h) * vocab
    chosen = jnp.sum(jnp.where(column == cand, logits, 0.0), axis=1, keepdims=True)
    lane = lax.broadcasted_iota(jnp.int32, (logits.shape[0], 128), 1)
    packed = jnp.where(lane == 0, peak, jnp.where(lane == 1, mass, chosen)).T
    vst1[0] = packed[0:8]

    def merged(ref, count):
        top = ref[0, 0:1, :]
        for k in range(1, count):
            top = jnp.maximum(top, ref[k, 0:1, :])
        total = jnp.zeros_like(top)
        picked = jnp.zeros_like(top)
        for k in range(count):
            total = total + ref[k, 1:2, :] * jnp.exp(ref[k, 0:1, :] - top)
            picked = picked + ref[k, 2:3, :]
        return top, total, picked

    copies = [
        send(vst1.at[0], vst1.at[k], v1_ss.at[k], v1_rs.at[k], {"seq": seq_peer(k)})
        for k in range(1, seq)
    ]
    for copy in copies:
        copy.wait_recv()
    top, total, picked = merged(vst1, seq)
    row = lax.broadcasted_iota(jnp.int32, (8, 128), 0)
    vst2[0] = jnp.where(row == 0, top, jnp.where(row == 1, total, picked))
    copies = [
        send(vst2.at[0], vst2.at[k], v2_ss.at[k], v2_rs.at[k], {"head": head_peer(k)})
        for k in range(1, head)
    ]
    for copy in copies:
        copy.wait_recv()
    top, total, picked = merged(vst2, head)
    con_ref[...] = picked - (top + jnp.log(total)) - amateur_ref[...]
    for copy in pending:
        copy.wait_send()


def tail(acc, stats, out_weight, residual, norm_gain, vocab_weight, candidates, amateur, head):
    seq, _, width = acc.shape
    depth, cols = out_weight.shape
    share = cols // head
    vocab = vocab_weight.shape[1]
    count = residual.shape[0]
    nodes = count // 2
    chips = seq // 2
    slots = min(7, seq * head // 2)
    dma = pltpu.SemaphoreType.DMA
    vmem = pl.BlockSpec(memory_space=pltpu.VMEM)
    hbm = pl.BlockSpec(memory_space=pl.ANY)
    bf16, f32 = jnp.bfloat16, jnp.float32
    hidden, contrast = pl.pallas_call(
        functools.partial(tail_kernel, seq, head, slots, nodes),
        in_specs=[hbm, hbm, hbm, vmem, vmem, hbm, vmem, vmem],
        out_specs=[vmem, vmem],
        out_shape=[
            jax.ShapeDtypeStruct((count, share), bf16),
            jax.ShapeDtypeStruct((1, count), f32),
        ],
        scratch_shapes=[
            pltpu.VMEM((seq, HD, width), bf16),
            pltpu.VMEM((seq, 8, width), f32),
            pltpu.VMEM((count, depth), bf16),
            pltpu.VMEM((head, depth, share), bf16),
            pltpu.VMEM((slots, 2 * share, vocab), bf16),
            pltpu.VMEM((head, count, share), bf16),
            pltpu.VMEM((head, count, share), bf16),
            pltpu.VMEM((chips, 2, head, count, share), bf16),
            pltpu.VMEM((count, vocab), f32),
            pltpu.VMEM((seq, 8, 128), f32),
            pltpu.VMEM((head, 8, 128), f32),
            dma((2,)), dma((head,)), dma((slots, 2)),
            dma((seq,)), dma((seq,)), dma((seq,)), dma((seq,)),
            dma((seq,)), dma((seq,)), dma((head,)), dma((head,)),
            dma((head,)), dma((head,)),
            dma((chips, head)), dma((chips, head)), dma((chips, head)), dma((chips, head)),
            dma((seq,)), dma((seq,)), dma((head,)), dma((head,)),
        ],
        compiler_params=pltpu.CompilerParams(
            collective_id=0, has_side_effects=True, vmem_limit_bytes=60 * 2**20
        ),
        cost_estimate=pl.CostEstimate(
            flops=2 * count * (depth * cols + vocab_weight.size),
            bytes_accessed=2 * (out_weight.size + vocab_weight.size),
            transcendentals=count * vocab,
        ),
    )(
        acc, stats, out_weight, residual, norm_gain[None, :], vocab_weight,
        candidates[None, :], amateur[None, :],
    )
    return hidden, contrast[0]


def solution(mesh):
    seq, head = mesh.shape["seq"], mesh.shape["head"]

    def body(
        queries, cache_keys, cache_values, tree_keys, tree_values, ancestors, filled_extents,
        out_weight, residual, norm_gain, vocab_weight, candidates, amateur,
    ):
        acc, stats = attention(
            queries, cache_keys, cache_values, tree_keys, tree_values, ancestors,
            filled_extents, seq,
        )
        return tail(
            acc, stats, out_weight, residual, norm_gain, vocab_weight, candidates, amateur, head
        )

    in_specs = (
        P(None, "head"),
        P(None, "seq", "head"),
        P(None, "seq", "head"),
        P(None, "head"),
        P(None, "head"),
        P(),
        P(),
        P("head", "seq"),
        P(None, "seq"),
        P(),
        P(None, ("seq", "head")),
        P(),
        P(),
    )
    out_specs = (P(None, ("seq", "head")), P())
    return jax.shard_map(body, mesh=mesh, in_specs=in_specs, out_specs=out_specs, check_vma=False)
```
